32 devices in a mesh: row: 2 (over x), col: 4 (over y, core), slab: 4 (over z).
Axes of the slice: x: 2, y: 2, z: 4, core: 2. Of those that a mesh axis runs over, the one named last changes fastest.
Arguments:
- inputs: bfloat16 [32, 64, 6144], P('col', None, ('row', 'slab')), may hold values from -6 to 6
- first_weight: bfloat16 [3, 3, 6144, 6144], P(None, None, ('row', 'slab'), 'col'), may hold values from -0.02734375 to 0.02734375
- second_weight: bfloat16 [3, 3, 6144, 6144], P(None, None, 'col', ('row', 'slab')), may hold values from -0.02734375 to 0.02734375
Outputs:
- result: bfloat16 [32, 64, 6144], P('col', None, ('row', 'slab'))
The draws below stay inside these ranges and needn't reach their ends.
All inputs are finite; a program needn't handle non-finite values.
Results may differ from the reference program's by a relative error of at most 0.015.
Values may be sent and summed in bfloat16 or wider, within the bound.
A program may use at most 192 MiB of HBM per device.

```python
import jax
import jax.numpy as jnp
from jax import lax

C = 6144
H = 32
W = 64


def level_of(stream_key, dims, shards, smallest, high):
    def one(position, shards_of):
        steps = jax.random.uniform(jax.random.fold_in(jax.random.fold_in(stream_key, 6), position), (shards_of,), jnp.float32, smallest / len(shards), high / len(shards))
        return jnp.repeat(jnp.exp(steps), dims[position] // shards_of).reshape((-1,) + (1,) * (len(dims) - position - 1))

    loudness = one(*shards[0])
    for cut in shards[1:]:
        loudness = loudness * one(*cut)
    return loudness


def bell_draw(own_key, shape, spread, most, cuts=(), dtype=jnp.bfloat16):
    drawn = spread * jax.random.normal(own_key, shape, jnp.float32)
    if cuts:
        drawn = drawn * level_of(own_key, shape, cuts, -0.22, 0.18)
    return jnp.clip(drawn, -most, most).astype(dtype)


def setup_inputs(seed: int = 0) -> dict:
    arg_keys = jax.random.split(jax.random.key(seed), 4)
    return {
        "inputs": bell_draw(arg_keys[0], (H, W, C), 1.0, 6.0, ((0, 4), (2, 8))),
        "first_weight": bell_draw(arg_keys[1], (3, 3, C, C), (9 * C) ** -0.5, 0.02734375, ((2, 8), (3, 4))),
        "second_weight": bell_draw(arg_keys[2], (3, 3, C, C), (9 * C) ** -0.5, 0.02734375, ((2, 4), (3, 8))),
    }


def convolve(image, kernel):
    output = lax.conv_general_dilated(image[None].astype(jnp.float32), kernel.astype(jnp.float32), (1, 1), ((1, 1), (1, 1)), dimension_numbers=("NHWC", "HWIO", "NHWC"), precision=lax.Precision.HIGHEST)
    return output[0]


def reference(inputs, first_weight, second_weight):
    first = convolve(inputs, first_weight)
    hidden = jax.nn.silu(first).astype(jnp.bfloat16)
    second = convolve(hidden, second_weight)
    return (inputs.astype(jnp.float32) + second).astype(jnp.bfloat16)
```

```python
import functools

import jax
import jax.numpy as jnp
from jax import lax
from jax.experimental import pallas as pl
from jax.experimental.pallas import tpu as pltpu
from jax.sharding import PartitionSpec as P

CHUNKS = 3


def tile_of(size):
    return 256 if size % 256 == 0 else size


def conv_kernel(height, width, with_total, x_ref, w_ref, *rest):
    if with_total:
        total_ref, out_ref, wide = rest
    else:
        out_ref, wide = rest
    depth = x_ref.shape[1]

    @pl.when(pl.program_id(0) == 0)
    def _():
        edge = jnp.zeros((width, 3 * depth), wide.dtype)
        wide[0:width, :] = edge
        wide[(height + 1) * width : (height + 2) * width, :] = edge

        @pl.loop(0, height)
        def _(line):
            start = pl.multiple_of(line * width, width)
            there = pl.multiple_of((line + 1) * width, width)
            block = x_ref[pl.ds(start, width), :]
            long = block.astype(jnp.float32)
            place = lax.broadcasted_iota(jnp.int32, (width, depth), 0)
            before = jnp.where(place == 0, 0.0, pltpu.roll(long, 1, 0))
            after = jnp.where(place == width - 1, 0.0, pltpu.roll(long, width - 1, 0))
            whole = jnp.concatenate([before.astype(wide.dtype), block, after.astype(wide.dtype)], axis=1)
            wide[pl.ds(there, width), :] = whole

    pixels = height * width
    step = 1024

    @pl.loop(0, pixels // step)
    def _(part):
        base = pl.multiple_of(part * step, step)
        sums = None
        for vertical in range(3):
            kernel = w_ref[vertical].reshape(3 * depth, w_ref.shape[3])
            term = jnp.dot(
                wide[pl.ds(pl.multiple_of(base + vertical * width, width), step), :],
                kernel,
                preferred_element_type=jnp.float32,
            )
            sums = term if sums is None else sums + term
        if with_total:
            sums = sums + total_ref[pl.ds(base, step), :]
        out_ref[pl.ds(base, step), :] = sums.astype(out_ref.dtype)


def conv(x, weight, height, width, in_chunk, in_size, out_start, out_size, total, out_dtype):
    pixels = height * width
    tile = tile_of(out_size)
    first_tile = out_start // tile
    in_specs = [
        pl.BlockSpec((pixels, in_size), lambda j: (0, 0), pipeline_mode=pl.Buffered(1)),
        pl.BlockSpec((3, 3, in_size, tile), lambda j: (0, 0, in_chunk, first_tile + j)),
    ]
    args = [x, weight]
    if total is not None:
        in_specs.append(pl.BlockSpec((pixels, tile), lambda j: (0, j)))
        args.append(total)
    return pl.pallas_call(
        functools.partial(conv_kernel, height, width, total is not None),
        grid=(out_size // tile,),
        in_specs=in_specs,
        out_specs=pl.BlockSpec((pixels, tile), lambda j: (0, j)),
        out_shape=jax.ShapeDtypeStruct((pixels, out_size), out_dtype),
        scratch_shapes=[pltpu.VMEM(((height + 2) * width, 3 * in_size), jnp.bfloat16)],
        compiler_params=pltpu.CompilerParams(
            dimension_semantics=("arbitrary",), vmem_limit_bytes=48 * 1024 * 1024
        ),
        cost_estimate=pl.CostEstimate(
            flops=2 * pixels * 9 * in_size * out_size,
            bytes_accessed=2 * (9 * in_size * out_size + pixels * in_size + pixels * out_size),
            transcendentals=0,
        ),
    )(*args)


def local(inputs, first_weight, second_weight):
    full_input = lax.all_gather(inputs, "col", axis=0, tiled=True)
    height, width, depth = full_input.shape
    pixels = height * width
    flat = full_input.reshape(pixels, depth)
    out_first = first_weight.shape[3]
    out_second = second_weight.shape[3]
    size = out_first // CHUNKS
    hiddens = []
    for chunk in range(CHUNKS):
        first = conv(flat, first_weight, height, width, 0, depth, chunk * size, size, None, jnp.bfloat16)
        first = lax.psum_scatter(first, ("row", "slab"), scatter_dimension=0, tiled=True)
        hidden = jax.nn.silu(first.astype(jnp.float32)).astype(jnp.bfloat16)
        hiddens.append(lax.all_gather(hidden, ("row", "slab"), axis=0, tiled=True))
    total = None
    for chunk in range(CHUNKS):
        last = chunk == CHUNKS - 1
        total = conv(
            hiddens[chunk], second_weight, height, width, chunk, size, 0, out_second, total,
            jnp.bfloat16 if last else jnp.float32,
        )
    second = lax.psum_scatter(total, "col", scatter_dimension=0, tiled=True).astype(jnp.float32)
    combined = inputs.astype(jnp.float32) + second.reshape(inputs.shape)
    return combined.astype(jnp.bfloat16)


def solution(mesh):
    in_specs = (
        P("col", None, ("row", "slab")),
        P(None, None, ("row", "slab"), "col"),
        P(None, None, "col", ("row", "slab")),
    )
    out_specs = P("col", None, ("row", "slab"))
    return jax.shard_map(local, mesh=mesh, in_specs=in_specs, out_specs=out_specs, check_vma=False)
```

```python
import functools

import jax
import jax.numpy as jnp
from jax import lax
from jax.experimental import pallas as pl
from jax.experimental.pallas import tpu as pltpu
from jax.sharding import PartitionSpec as P

CHUNKS = 3


def tile_of(size):
    return 256 if size % 256 == 0 else size


def conv_kernel(height, width, with_total, x_ref, w_ref, *rest):
    if with_total:
        total_ref, out_ref, wide = rest
    else:
        out_ref, wide = rest
    depth = x_ref.shape[1]

    @pl.when(pl.program_id(0) == 0)
    def _():
        edge = jnp.zeros((width, 3 * depth), wide.dtype)
        wide[0:width, :] = edge
        wide[(height + 1) * width : (height + 2) * width, :] = edge

        @pl.loop(0, height)
        def _(line):
            start = pl.multiple_of(line * width, width)
            there = pl.multiple_of((line + 1) * width, width)
            block = x_ref[pl.ds(start, width), :]
            long = block.astype(jnp.float32)
            place = lax.broadcasted_iota(jnp.int32, (width, depth), 0)
            before = jnp.where(place == 0, 0.0, pltpu.roll(long, 1, 0))
            after = jnp.where(place == width - 1, 0.0, pltpu.roll(long, width - 1, 0))
            whole = jnp.concatenate([before.astype(wide.dtype), block, after.astype(wide.dtype)], axis=1)
            wide[pl.ds(there, width), :] = whole

    pixels = height * width
    step = 1024

    @pl.loop(0, pixels // step)
    def _(part):
        base = pl.multiple_of(part * step, step)
        sums = None
        for vertical in range(3):
            kernel = w_ref[vertical].reshape(3 * depth, w_ref.shape[3])
            term = jnp.dot(
                wide[pl.ds(pl.multiple_of(base + vertical * width, width), step), :],
                kernel,
                preferred_element_type=jnp.float32,
            )
            sums = term if sums is None else sums + term
        if with_total:
            sums = sums + total_ref[pl.ds(base, step), :]
        out_ref[pl.ds(base, step), :] = sums.astype(out_ref.dtype)


def conv(x, weight, height, width, in_chunk, in_size, out_start, out_size, total, out_dtype):
    pixels = height * width
    tile = tile_of(out_size)
    first_tile = out_start // tile
    in_specs = [
        pl.BlockSpec((pixels, in_size), lambda j: (0, 0), pipeline_mode=pl.Buffered(1)),
        pl.BlockSpec((3, 3, in_size, tile), lambda j: (0, 0, in_chunk, first_tile + j)),
    ]
    args = [x, weight]
    if total is not None:
        in_specs.append(pl.BlockSpec((pixels, tile), lambda j: (0, j)))
        args.append(total)
    return pl.pallas_call(
        functools.partial(conv_kernel, height, width, total is not None),
        grid=(out_size // tile,),
        in_specs=in_specs,
        out_specs=pl.BlockSpec((pixels, tile), lambda j: (0, j)),
        out_shape=jax.ShapeDtypeStruct((pixels, out_size), out_dtype),
        scratch_shapes=[pltpu.VMEM(((height + 2) * width, 3 * in_size), jnp.bfloat16)],
        compiler_params=pltpu.CompilerParams(
            dimension_semantics=("arbitrary",), vmem_limit_bytes=48 * 1024 * 1024
        ),
        cost_estimate=pl.CostEstimate(
            flops=2 * pixels * 9 * in_size * out_size,
            bytes_accessed=2 * (9 * in_size * out_size + pixels * in_size + pixels * out_size),
            transcendentals=0,
        ),
    )(*args)


def shift(x, axis, sources, by):
    return lax.ppermute(x, axis, [(i, i + by) for i in sources])


def wide(value):
    return value.astype(jnp.float32)


def piece(pieces, index):
    n = pieces.shape[0]
    return lax.dynamic_index_in_dim(pieces, jnp.clip(index, 0, n - 1), 0, keepdims=False)


def cut(x, n):
    return x.reshape((n, x.shape[0] // n) + x.shape[1:])


def line_sends(pieces, axis, step):
    n, me = pieces.shape[0], lax.axis_index(axis)
    return piece(pieces, me + n - step), piece(pieces, me - n + step)


def line_move(sends, axis, step):
    n = lax.axis_size(axis)
    up = shift(sends[0], axis, range(0, step), 1)
    return up, shift(sends[1], axis, range(n - step, n), -1)


def line_finish(pieces, got, axis):
    n, me = pieces.shape[0], lax.axis_index(axis)
    for step in range(2, n):
        sends = [
            (wide(mine) + wide(came)).astype(pieces.dtype)
            for mine, came in zip(line_sends(pieces, axis, step), got)
        ]
        got = line_move(sends, axis, step)
    return wide(piece(pieces, me)) + wide(got[0]) + wide(got[1])


def scatter_sum(x, axis):
    n = lax.axis_size(axis)
    if n > 4 or n < 3:
        return lax.psum_scatter(x, axis, scatter_dimension=0, tiled=True)
    pieces = cut(x, n)
    got = line_move(line_sends(pieces, axis, 1), axis, 1)
    return line_finish(pieces, got, axis).astype(x.dtype)


def gather(x, axis):
    n = lax.axis_size(axis)
    me = lax.axis_index(axis)
    if n > 4:
        return lax.all_gather(x, axis, axis=0, tiled=True)
    if n == 2:
        other = lax.ppermute(x, axis, [(0, 1), (1, 0)])
        line = [other, x, other]
    else:
        line = [x]
        up = down = x
        for step in range(1, n):
            up = shift(up, axis, range(step - 1, n - 1), 1)
            down = shift(down, axis, range(1, n - step + 1), -1)
            line = [up] + line + [down]
    size = x.shape[0]
    return lax.dynamic_slice_in_dim(jnp.concatenate(line, axis=0), (n - 1 - me) * size, n * size, 0)


def flip(x, axis, bit):
    return lax.ppermute(x, axis, [(i, i ^ bit) for i in range(lax.axis_size(axis))])


def gather_col(x):
    if lax.axis_size("col") != 4:
        return lax.all_gather(x, "col", axis=0, tiled=True)
    me = lax.axis_index("col")
    core, far = me % 2, me // 2
    beside = flip(x, "col", 1)
    across = flip(x, "col", 2)
    corner = flip(across, "col", 1)

    def pair(mine, other):
        return jnp.where(core == 0, jnp.stack([mine, other]), jnp.stack([other, mine]))

    near, away = pair(x, beside), pair(across, corner)
    both = jnp.where(far == 0, jnp.stack([near, away]), jnp.stack([away, near]))
    return both.reshape((4 * x.shape[0],) + x.shape[1:])


def scatter_col(x):
    if lax.axis_size("col") != 4:
        return lax.psum_scatter(x, "col", scatter_dimension=0, tiled=True).astype(jnp.float32)
    me = lax.axis_index("col")
    core, far = me % 2, me // 2
    rows = x.shape[0] // 4
    pieces = x.reshape((2, 2, rows) + x.shape[1:])

    def pick(array, index, axis):
        return lax.dynamic_index_in_dim(array, index, axis, keepdims=False)

    other = flip(pick(pieces, 1 - core, 1), "col", 1)
    halves = (pick(pieces, core, 1).astype(jnp.float32) + other.astype(jnp.float32))
    sent = pick(halves, 1 - far, 0).astype(x.dtype)
    return pick(halves, far, 0) + flip(sent, "col", 2).astype(jnp.float32)


def finish(first):
    hidden = jax.nn.silu(first.astype(jnp.float32)).astype(jnp.bfloat16)
    return gather(hidden, "slab")


def after(values, *earlier):
    tied = lax.optimization_barrier((*values, *earlier))
    return tied[: len(values)]


def hidden_chunks(layer_one):
    if lax.axis_size("row") != 2 or lax.axis_size("slab") != 4:
        return [
            gather(finish(scatter_sum(scatter_sum(layer_one(chunk, ()), "row"), "slab")), "row")
            for chunk in range(CHUNKS)
        ]
    row = lax.axis_index("row")

    def halves(first):
        pieces = cut(first, 2)
        return piece(pieces, row), piece(pieces, 1 - row)

    def exchange(sent):
        return lax.ppermute(sent, "row", [(0, 1), (1, 0)])

    def added(kept, other):
        return cut((wide(kept) + wide(other)).astype(kept.dtype), 4)

    kept0, sent0 = halves(layer_one(0, ()))
    other0 = exchange(sent0)
    kept1, sent1 = halves(layer_one(1, (sent0,)))
    other1 = exchange(sent1)
    sum0 = added(kept0, other0)
    sends0 = line_sends(sum0, "slab", 1)
    got0 = line_move(sends0, "slab", 1)
    kept2, sent2 = halves(layer_one(2, (sent1, *sends0)))
    other2 = exchange(sent2)
    up0, down0, other1 = after((*got0, other1), sent2)
    sum1 = added(kept1, other1)
    sends1 = line_sends(sum1, "slab", 1)
    got1 = line_move(sends1, "slab", 1)
    first0 = line_finish(sum0, (up0, down0), "slab")
    parts0 = finish(first0)
    parts1 = finish(line_finish(sum1, got1, "slab"))
    (other2,) = after((other2,), parts0)
    sum2 = added(kept2, other2)
    got2 = line_move(line_sends(sum2, "slab", 1), "slab", 1)
    parts2 = finish(line_finish(sum2, got2, "slab"))
    return [gather(part, "row") for part in (parts0, parts1, parts2)]


def local(inputs, first_weight, second_weight):
    full_input = gather_col(inputs)
    height, width, depth = full_input.shape
    pixels = height * width
    flat = full_input.reshape(pixels, depth)
    out_first = first_weight.shape[3]
    out_second = second_weight.shape[3]
    size = out_first // CHUNKS

    def layer_one(chunk, earlier):
        (source,) = after((flat,), *earlier) if earlier else (flat,)
        return conv(source, first_weight, height, width, 0, depth, chunk * size, size, None, jnp.bfloat16)

    hiddens = hidden_chunks(layer_one)
    total = None
    for chunk in range(CHUNKS):
        last = chunk == CHUNKS - 1
        total = conv(
            hiddens[chunk], second_weight, height, width, chunk, size, 0, out_second, total,
            jnp.bfloat16 if last else jnp.float32,
        )
    second = scatter_col(total)
    combined = inputs.astype(jnp.float32) + second.reshape(inputs.shape)
    return combined.astype(jnp.bfloat16)


def solution(mesh):
    in_specs = (
        P("col", None, ("row", "slab")),
        P(None, None, ("row", "slab"), "col"),
        P(None, None, "col", ("row", "slab")),
    )
    out_specs = P("col", None, ("row", "slab"))
    return jax.shard_map(local, mesh=mesh, in_specs=in_specs, out_specs=out_specs, check_vma=False)
```

```python
import functools

import jax
import jax.numpy as jnp
from jax import lax
from jax.experimental import pallas as pl
from jax.experimental.pallas import tpu as pltpu
from jax.sharding import PartitionSpec as P

CHUNKS = 3


def tile_of(size):
    return 256 if size % 256 == 0 else size


def conv_kernel(height, width, with_total, x_ref, w_ref, *rest):
    if with_total:
        total_ref, out_ref, wide = rest
    else:
        out_ref, wide = rest
    depth = x_ref.shape[1]

    @pl.when(pl.program_id(0) == 0)
    def _():
        edge = jnp.zeros((width, 3 * depth), wide.dtype)
        wide[0:width, :] = edge
        wide[(height + 1) * width : (height + 2) * width, :] = edge

        @pl.loop(0, height)
        def _(line):
            start = pl.multiple_of(line * width, width)
            there = pl.multiple_of((line + 1) * width, width)
            block = x_ref[pl.ds(start, width), :]
            long = block.astype(jnp.float32)
            place = lax.broadcasted_iota(jnp.int32, (width, depth), 0)
            before = jnp.where(place == 0, 0.0, pltpu.roll(long, 1, 0))
            after = jnp.where(place == width - 1, 0.0, pltpu.roll(long, width - 1, 0))
            whole = jnp.concatenate([before.astype(wide.dtype), block, after.astype(wide.dtype)], axis=1)
            wide[pl.ds(there, width), :] = whole

    pixels = height * width
    step = 1024

    @pl.loop(0, pixels // step)
    def _(part):
        base = pl.multiple_of(part * step, step)
        sums = None
        for vertical in range(3):
            kernel = w_ref[vertical].reshape(3 * depth, w_ref.shape[3])
            term = jnp.dot(
                wide[pl.ds(pl.multiple_of(base + vertical * width, width), step), :],
                kernel,
                preferred_element_type=jnp.float32,
            )
            sums = term if sums is None else sums + term
        if with_total:
            sums = sums + total_ref[pl.ds(base, step), :]
        out_ref[pl.ds(base, step), :] = sums.astype(out_ref.dtype)


def conv(x, weight, height, width, in_chunk, in_size, out_start, out_size, total, out_dtype):
    pixels = height * width
    tile = tile_of(out_size)
    first_tile = out_start // tile
    in_specs = [
        pl.BlockSpec((pixels, in_size), lambda j: (0, 0), pipeline_mode=pl.Buffered(1)),
        pl.BlockSpec((3, 3, in_size, tile), lambda j: (0, 0, in_chunk, first_tile + j)),
    ]
    args = [x, weight]
    if total is not None:
        in_specs.append(pl.BlockSpec((pixels, tile), lambda j: (0, first_tile + j)))
        args.append(total)
    return pl.pallas_call(
        functools.partial(conv_kernel, height, width, total is not None),
        grid=(out_size // tile,),
        in_specs=in_specs,
        out_specs=pl.BlockSpec((pixels, tile), lambda j: (0, j)),
        out_shape=jax.ShapeDtypeStruct((pixels, out_size), out_dtype),
        scratch_shapes=[pltpu.VMEM(((height + 2) * width, 3 * in_size), jnp.bfloat16)],
        compiler_params=pltpu.CompilerParams(
            dimension_semantics=("arbitrary",), vmem_limit_bytes=48 * 1024 * 1024
        ),
        cost_estimate=pl.CostEstimate(
            flops=2 * pixels * 9 * in_size * out_size,
            bytes_accessed=2 * (9 * in_size * out_size + pixels * in_size + pixels * out_size),
            transcendentals=0,
        ),
    )(*args)


def wide(value):
    return value.astype(jnp.float32)


def piece(pieces, index, axis=0):
    return lax.dynamic_index_in_dim(pieces, index, axis, keepdims=False)


def cut(x, n):
    return x.reshape((n, x.shape[0] // n) + x.shape[1:])


def flip(x, axis, bit):
    return lax.ppermute(x, axis, [(i, i ^ bit) for i in range(lax.axis_size(axis))])


def joined(mine, other, bit, axis):
    return jnp.where(bit == 0, jnp.stack([mine, other], axis), jnp.stack([other, mine], axis))


def bits(axis):
    me = lax.axis_index(axis)
    return me % 2, me // 2


def gather_col(x):
    if lax.axis_size("col") != 4:
        return lax.all_gather(x, "col", axis=0, tiled=True)
    core, far = bits("col")
    beside = flip(x, "col", 1)
    across = flip(x, "col", 2)
    corner = flip(across, "col", 1)
    both = joined(joined(x, beside, core, 0), joined(across, corner, core, 0), far, 0)
    return both.reshape((4 * x.shape[0],) + x.shape[1:])


def scatter_col(x):
    if lax.axis_size("col") != 4:
        return wide(lax.psum_scatter(x, "col", scatter_dimension=0, tiled=True)), None
    core, far = bits("col")
    pieces = cut(cut(x, 4), 2)
    other = flip(piece(pieces, 1 - core, 1), "col", 1)
    halves = wide(piece(pieces, core, 1)) + wide(other)
    sent = piece(halves, 1 - far).astype(x.dtype)
    return piece(halves, far), sent


def silu(value):
    return jax.nn.silu(value).astype(jnp.bfloat16)


def after(values, *earlier):
    tied = lax.optimization_barrier((*values, *earlier))
    return tied[: len(values)]


def hidden_chunks(layer_one):
    if lax.axis_size("row") != 2 or lax.axis_size("slab") != 4:
        both = ("row", "slab")
        return [
            lax.all_gather(
                silu(wide(lax.psum_scatter(layer_one(chunk, ()), both, scatter_dimension=0, tiled=True))),
                both, axis=0, tiled=True,
            )
            for chunk in range(CHUNKS)
        ]
    row = lax.axis_index("row")
    low, high = bits("slab")

    def halves(first):
        pieces = cut(first, 2)
        return piece(pieces, row), piece(pieces, 1 - row)

    def near(kept, other):
        total = cut(cut((wide(kept) + wide(other)).astype(kept.dtype), 4), 2)
        return piece(total, low, 1), piece(total, 1 - low, 1)

    def distant(kept, other):
        total = (wide(kept) + wide(other)).astype(kept.dtype)
        return piece(total, high), piece(total, 1 - high)

    def spread(kept, other):
        kept, sent = distant(kept, other)
        hidden = silu(wide(kept) + wide(flip(sent, "slab", 2)))
        pair = joined(hidden, flip(hidden, "slab", 2), high, 0)
        quad = joined(pair, flip(pair, "slab", 1), low, 1)
        return hidden, quad.reshape((-1, quad.shape[-1]))

    kept0, sent0 = halves(layer_one(0, ()))
    other0 = flip(sent0, "row", 1)
    kept1, sent1 = halves(layer_one(1, (sent0,)))
    other1 = flip(sent1, "row", 1)
    kept0, sent0 = near(kept0, other0)
    other0 = flip(sent0, "slab", 1)
    kept2, sent2 = halves(layer_one(2, (sent1, sent0)))
    other2 = flip(sent2, "row", 1)
    other0, other1 = after((other0, other1), sent2)
    kept1, sent1 = near(kept1, other1)
    other1 = flip(sent1, "slab", 1)
    hidden0, quad0 = spread(kept0, other0)
    hidden1, quad1 = spread(kept1, other1)
    (other2,) = after((other2,), hidden0)
    kept2, sent2 = near(kept2, other2)
    hidden2, quad2 = spread(kept2, flip(sent2, "slab", 1))
    return [
        joined(quad, flip(quad, "row", 1), row, 0).reshape((-1, quad.shape[-1]))
        for quad in (quad0, quad1, quad2)
    ]


def local(inputs, first_weight, second_weight):
    full_input = gather_col(inputs)
    height, width, depth = full_input.shape
    pixels = height * width
    flat = full_input.reshape(pixels, depth)
    out_first = first_weight.shape[3]
    out_second = second_weight.shape[3]
    size = out_first // CHUNKS

    def layer_one(chunk, earlier):
        (source,) = after((flat,), *earlier) if earlier else (flat,)
        return conv(source, first_weight, height, width, 0, depth, chunk * size, size, None, jnp.bfloat16)

    hiddens = hidden_chunks(layer_one)
    total = None
    for chunk in range(CHUNKS - 1):
        total = conv(hiddens[chunk], second_weight, height, width, chunk, size, 0, out_second, total, jnp.float32)
    split = 512 if out_second % 256 == 0 and out_second > 512 else out_second
    parts = []
    for start, end in ((0, split), (split, out_second)):
        if start == end:
            continue
        part = conv(
            hiddens[-1], second_weight, height, width, CHUNKS - 1, size, start, end - start, total, jnp.bfloat16
        )
        second, sent = scatter_col(part)
        if sent is not None:
            second = second + wide(flip(sent, "col", 2))
            (total,) = after((total,), sent)
        second = second.reshape(inputs.shape[:2] + (end - start,))
        parts.append((wide(inputs[:, :, start:end]) + second).astype(jnp.bfloat16))
    return jnp.concatenate(parts, axis=2)


def solution(mesh):
    in_specs = (
        P("col", None, ("row", "slab")),
        P(None, None, ("row", "slab"), "col"),
        P(None, None, "col", ("row", "slab")),
    )
    out_specs = P("col", None, ("row", "slab"))
    return jax.shard_map(local, mesh=mesh, in_specs=in_specs, out_specs=out_specs, check_vma=False)
```

```python
import functools

import jax
import jax.numpy as jnp
from jax import lax
from jax.experimental import pallas as pl
from jax.experimental.pallas import tpu as pltpu
from jax.sharding import PartitionSpec as P

CHUNKS = 3


def tile_of(size):
    return 256 if size % 256 == 0 else size


def conv_kernel(height, width, with_total, x_ref, w_ref, *rest):
    if with_total:
        total_ref, out_ref, wide = rest
    else:
        out_ref, wide = rest
    depth = x_ref.shape[1]

    @pl.when(pl.program_id(0) == 0)
    def _():
        edge = jnp.zeros((width, 3 * depth), wide.dtype)
        wide[0:width, :] = edge
        wide[(height + 1) * width : (height + 2) * width, :] = edge

        @pl.loop(0, height)
        def _(line):
            start = pl.multiple_of(line * width, width)
            there = pl.multiple_of((line + 1) * width, width)
            block = x_ref[pl.ds(start, width), :]
            long = block.astype(jnp.float32)
            place = lax.broadcasted_iota(jnp.int32, (width, depth), 0)
            before = jnp.where(place == 0, 0.0, pltpu.roll(long, 1, 0))
            after = jnp.where(place == width - 1, 0.0, pltpu.roll(long, width - 1, 0))
            whole = jnp.concatenate([before.astype(wide.dtype), block, after.astype(wide.dtype)], axis=1)
            wide[pl.ds(there, width), :] = whole

    pixels = height * width
    step = 1024

    @pl.loop(0, pixels // step)
    def _(part):
        base = pl.multiple_of(part * step, step)
        sums = None
        for vertical in range(3):
            kernel = w_ref[vertical].reshape(3 * depth, w_ref.shape[3])
            term = jnp.dot(
                wide[pl.ds(pl.multiple_of(base + vertical * width, width), step), :],
                kernel,
                preferred_element_type=jnp.float32,
            )
            sums = term if sums is None else sums + term
        if with_total:
            sums = sums + total_ref[pl.ds(base, step), :]
        out_ref[pl.ds(base, step), :] = sums.astype(out_ref.dtype)


def conv(x, weight, height, width, in_chunk, in_size, out_start, out_size, total, out_dtype):
    pixels = height * width
    tile = tile_of(out_size)
    first_tile = out_start // tile
    in_specs = [
        pl.BlockSpec((pixels, in_size), lambda j: (0, 0), pipeline_mode=pl.Buffered(1)),
        pl.BlockSpec((3, 3, in_size, tile), lambda j: (0, 0, in_chunk, first_tile + j)),
    ]
    args = [x, weight]
    if total is not None:
        in_specs.append(pl.BlockSpec((pixels, tile), lambda j: (0, first_tile + j)))
        args.append(total)
    return pl.pallas_call(
        functools.partial(conv_kernel, height, width, total is not None),
        grid=(out_size // tile,),
        in_specs=in_specs,
        out_specs=pl.BlockSpec((pixels, tile), lambda j: (0, j)),
        out_shape=jax.ShapeDtypeStruct((pixels, out_size), out_dtype),
        scratch_shapes=[pltpu.VMEM(((height + 2) * width, 3 * in_size), jnp.bfloat16)],
        compiler_params=pltpu.CompilerParams(
            dimension_semantics=("arbitrary",), vmem_limit_bytes=48 * 1024 * 1024
        ),
        cost_estimate=pl.CostEstimate(
            flops=2 * pixels * 9 * in_size * out_size,
            bytes_accessed=2 * (9 * in_size * out_size + pixels * in_size + pixels * out_size),
            transcendentals=0,
        ),
    )(*args)


def wide(value):
    return value.astype(jnp.float32)


def piece(pieces, index, axis=0):
    return lax.dynamic_index_in_dim(pieces, index, axis, keepdims=False)


def cut(x, n):
    return x.reshape((n, x.shape[0] // n) + x.shape[1:])


def flip(x, axis, bit):
    return lax.ppermute(x, axis, [(i, i ^ bit) for i in range(lax.axis_size(axis))])


def joined(mine, other, bit, axis):
    return jnp.where(bit == 0, jnp.stack([mine, other], axis), jnp.stack([other, mine], axis))


def bits(axis):
    me = lax.axis_index(axis)
    return me % 2, me // 2


def gather_col(x):
    if lax.axis_size("col") != 4:
        return lax.all_gather(x, "col", axis=0, tiled=True)
    core, far = bits("col")
    beside = flip(x, "col", 1)
    across = flip(x, "col", 2)
    corner = flip(across, "col", 1)
    both = joined(joined(x, beside, core, 0), joined(across, corner, core, 0), far, 0)
    return both.reshape((4 * x.shape[0],) + x.shape[1:])


def scatter_col(x):
    if lax.axis_size("col") != 4:
        return wide(lax.psum_scatter(x, "col", scatter_dimension=0, tiled=True)), None
    core, far = bits("col")
    pieces = cut(cut(x, 4), 2)
    other = flip(piece(pieces, 1 - core, 1), "col", 1)
    halves = wide(piece(pieces, core, 1)) + wide(other)
    sent = piece(halves, 1 - far).astype(x.dtype)
    return piece(halves, far), sent


def silu(value):
    return jax.nn.silu(value).astype(jnp.bfloat16)


def after(values, *earlier):
    tied = lax.optimization_barrier((*values, *earlier))
    return tied[: len(values)]


def hidden_chunks(layer_one):
    if lax.axis_size("row") != 2 or lax.axis_size("slab") != 4:
        both = ("row", "slab")
        return (), (), [
            lax.all_gather(
                silu(wide(lax.psum_scatter(layer_one(chunk, ()), both, scatter_dimension=0, tiled=True))),
                both, axis=0, tiled=True,
            )
            for chunk in range(CHUNKS)
        ]
    row = lax.axis_index("row")
    low, high = bits("slab")

    def halves(first):
        pieces = cut(first, 2)
        return piece(pieces, row), piece(pieces, 1 - row)

    def near(kept, other):
        total = cut(cut((wide(kept) + wide(other)).astype(kept.dtype), 4), 2)
        return piece(total, low, 1), piece(total, 1 - low, 1)

    def distant(kept, other):
        total = (wide(kept) + wide(other)).astype(kept.dtype)
        return piece(total, high), piece(total, 1 - high)

    def spread(kept, other):
        kept, sent = distant(kept, other)
        hidden = silu(wide(kept) + wide(flip(sent, "slab", 2)))
        pair = joined(hidden, flip(hidden, "slab", 2), high, 0)
        quad = joined(pair, flip(pair, "slab", 1), low, 1)
        return hidden, quad.reshape((-1, quad.shape[-1]))

    kept0, sent0 = halves(layer_one(0, ()))
    other0 = flip(sent0, "row", 1)
    kept1, sent1 = halves(layer_one(1, (sent0,)))
    other1 = flip(sent1, "row", 1)
    kept0, sent0 = near(kept0, other0)
    other0 = flip(sent0, "slab", 1)
    kept2, sent2 = halves(layer_one(2, (sent1, sent0)))
    other2 = flip(sent2, "row", 1)
    other0, other1 = after((other0, other1), sent2)
    kept1, sent1 = near(kept1, other1)
    other1 = flip(sent1, "slab", 1)
    hidden0, quad0 = spread(kept0, other0)
    hidden1, quad1 = spread(kept1, other1)
    (other2,) = after((other2,), quad0, hidden1)
    kept2, sent2 = near(kept2, other2)
    hidden2, quad2 = spread(kept2, flip(sent2, "slab", 1))
    return (hidden2,), (quad2,), [
        joined(quad, flip(quad, "row", 1), row, 0).reshape((-1, quad.shape[-1]))
        for quad in (quad0, quad1, quad2)
    ]


def local(inputs, first_weight, second_weight):
    full_input = gather_col(inputs)
    height, width, depth = full_input.shape
    pixels = height * width
    flat = full_input.reshape(pixels, depth)
    out_first = first_weight.shape[3]
    out_second = second_weight.shape[3]
    size = out_first // CHUNKS

    def layer_one(chunk, earlier):
        (source,) = after((flat,), *earlier) if earlier else (flat,)
        return conv(source, first_weight, height, width, 0, depth, chunk * size, size, None, jnp.bfloat16)

    *waits, hiddens = hidden_chunks(layer_one)
    total = None
    for chunk in range(CHUNKS - 1):
        (source,) = after((hiddens[chunk],), *waits[chunk]) if waits[chunk] else (hiddens[chunk],)
        total = conv(source, second_weight, height, width, chunk, size, 0, out_second, total, jnp.float32)
    split = 512 if out_second % 256 == 0 and out_second > 512 else out_second
    parts, came = [], ()
    for start, end in ((0, split), (split, out_second)):
        if start == end:
            continue
        part = conv(
            hiddens[-1], second_weight, height, width, CHUNKS - 1, size, start, end - start, total, jnp.bfloat16
        )
        if came:
            (part,) = after((part,), *came)
        second, sent = scatter_col(part)
        if sent is not None:
            got = flip(sent, "col", 2)
            second = second + wide(got)
            (total,) = after((total,), sent)
            came = (got,)
        second = second.reshape(inputs.shape[:2] + (end - start,))
        parts.append((wide(inputs[:, :, start:end]) + second).astype(jnp.bfloat16))
    return jnp.concatenate(parts, axis=2)


def solution(mesh):
    in_specs = (
        P("col", None, ("row", "slab")),
        P(None, None, ("row", "slab"), "col"),
        P(None, None, "col", ("row", "slab")),
    )
    out_specs = P("col", None, ("row", "slab"))
    return jax.shard_map(local, mesh=mesh, in_specs=in_specs, out_specs=out_specs, check_vma=False)
```
